32 devices in a mesh: segment: 2 (over x), dp: 16 (over z, y, core).
Axes of the slice: x: 2, y: 2, z: 4, core: 2. Of those that a mesh axis runs over, the one named last changes fastest.
Arguments:
- latents: bfloat16 [2, 2048, 3072], P(None, 'dp'), may hold values from -70 to 70
- proj: bfloat16 [2, 3072, 1536], P('segment', 'dp'), may hold values from -0.109375 to 0.109375
- temper: float32 [2, 12], P('segment'), may hold values from 0.3 to 24
- blocks: int32 [2, 32, 12, 2], P(None, 'dp'), may hold values from 0 to 5
Outputs:
- states: bfloat16 [2, 2, 2048, 3072], P('segment', None, 'dp')
The draws below stay inside these ranges and needn't reach their ends.
All inputs are finite; a program needn't handle non-finite values.
Results may differ from the reference program's by a relative error of at most 0.013.
Values may be sent and summed in bfloat16 or wider, within the bound.
A program may use at most 64 MiB of HBM per device.

```python
import math
import jax
import jax.numpy as jnp
from jax import lax

D = 3072
HEADS = 12
HD = 128
BLOCK = 64
SEL = 2
MICRO = 2
TOK_DEV = 128
WID = 1536
LAYERS = 2
TOKENS = 2048
SEQ = 2048
BPD = 2


def draw_latents(key, part):
    key_base = jax.random.fold_in(key, 0)
    base = jnp.clip(jax.random.normal(key_base, (MICRO, TOKENS, D), jnp.float32), -6.0, 6.0)
    result = base
    return result.astype(jnp.bfloat16)


def draw_temper(key, part):
    unit = jax.random.uniform(key, (LAYERS, HEADS), jnp.float32)
    upper = 2.0
    lower = 0.3
    return jnp.exp(jnp.log(lower) + unit * (jnp.log(upper) - jnp.log(lower)))


def place_ends(drawn, stream_key, low, top_value):
    longest = drawn.shape.index(max(drawn.shape))
    spots = []
    for shift in (0, 1):
        where = [jax.random.randint(jax.random.fold_in(stream_key, axis), (), 0, length) for axis, length in enumerate(drawn.shape)]
        where[longest] = (where[longest] + shift) % drawn.shape[longest]
        spots.append(tuple(where))
    return drawn.at[spots[0]].set(low).at[spots[1]].set(top_value)


def steps_of(stream_key, shape, shards, low, largest):
    def one(axis_at, blocks):
        steps = jax.random.uniform(jax.random.fold_in(jax.random.fold_in(stream_key, 6), axis_at), (blocks,), jnp.float32, low / len(shards), largest / len(shards))
        return jnp.repeat(jnp.exp(steps), shape[axis_at] // blocks).reshape((-1,) + (1,) * (len(shape) - axis_at - 1))

    level = one(*shards[0])
    for cut in shards[1:]:
        level = level * one(*cut)
    return level


def bell_draw(key, dims, width, bound, cuts=(), held_as=jnp.bfloat16):
    loudness = steps_of(key, dims, cuts, -0.22, 0.18) if cuts else 1.0
    array = jax.random.normal(key, dims, jnp.float32) * width * loudness
    return jnp.minimum(jnp.maximum(array, -bound), bound).astype(held_as)


def setup_inputs(seed: int = 0) -> dict:
    key_list = jax.random.split(jax.random.key(seed), 5)
    return {
        "latents": draw_latents(jax.random.fold_in(key_list[4], 71), 0),
        "proj": bell_draw(key_list[1], (LAYERS, D, WID), D ** -0.5, 0.109375, ((0, 2), (1, 16))),
        "temper": draw_temper(jax.random.fold_in(key_list[4], 71), 0),
        "blocks": place_ends(jax.random.randint(key_list[3], (MICRO, TOKENS // BLOCK, HEADS, SEL), 0, 3 * BPD), jax.random.fold_in(key_list[3], 1), 0, (3 * BPD) - 1).astype(jnp.int32),
    }


epsilon = 1e-06

def unit_heads(values, head_count):
    shaped = values.astype(jnp.float32).reshape(values.shape[:-1] + (head_count, -1))
    return (shaped * lax.rsqrt(lax.optimization_barrier(jnp.mean(shaped * shaped, axis=-1, keepdims=True)) + epsilon)).astype(jnp.bfloat16)

def layer(hidden, weight, temp, chosen):
    h_float = hidden.astype(jnp.float32)
    normed = (h_float * lax.rsqrt(lax.optimization_barrier(jnp.mean(h_float * h_float, axis=-1, keepdims=True)) + epsilon)).astype(jnp.bfloat16)
    values = jnp.dot(normed, weight, preferred_element_type=jnp.float32).astype(jnp.bfloat16)
    total_blocks = TOKENS // BLOCK
    per_dev = TOK_DEV // BLOCK
    seq_blocks = SEQ // BLOCK
    keys = unit_heads(values, HEADS).reshape(total_blocks, BLOCK, HEADS, HD)
    vals = values.reshape(total_blocks, BLOCK, HEADS, HD)
    query_block = jnp.arange(total_blocks, dtype=jnp.int32)
    absolute = ((query_block // per_dev - 1) * per_dev)[:, None, None] + chosen
    usable = (absolute >= 0) & (absolute < total_blocks) & (absolute // seq_blocks == (query_block // seq_blocks)[:, None, None])
    clipped = jnp.clip(absolute, 0, total_blocks - 1).astype(jnp.int32)
    head_index = jnp.arange(HEADS, dtype=jnp.int32)[None, :, None]
    keys_by_head = jnp.transpose(keys, (2, 0, 1, 3))
    vals_by_head = jnp.transpose(vals, (2, 0, 1, 3))
    key_pick = keys_by_head[head_index, clipped]
    val_pick = vals_by_head[head_index, clipped]
    score_scale = temp * (1.0 / math.sqrt(HD))
    keys_float = keys.astype(jnp.float32)
    own = jnp.einsum('bihd,bjhd->bhij', keys_float, keys_float) * score_scale[None, :, None, None]
    diag = jnp.eye(BLOCK, dtype=bool)
    own = jnp.where(diag[None, None], -jnp.inf, own)
    picked = jnp.einsum('bihd,bhsjd->bhisj', keys_float, key_pick.astype(jnp.float32)) * score_scale[None, :, None, None, None]
    same_block = absolute == query_block[:, None, None]
    keep = usable[:, :, None, :, None] & ~(same_block[:, :, None, :, None] & diag[None, None, :, None, :])
    picked = jnp.where(keep, picked, -jnp.inf)
    joined = jnp.concatenate([own, picked.reshape(total_blocks, HEADS, BLOCK, SEL * BLOCK)], axis=-1)
    weights = jax.nn.softmax(joined, axis=-1).astype(jnp.bfloat16)
    w_own = weights[..., :BLOCK].astype(jnp.float32)
    w_pick = weights[..., BLOCK:].reshape(total_blocks, HEADS, BLOCK, SEL, BLOCK).astype(jnp.float32)
    mixed = jnp.einsum('bhij,bjhd->bihd', w_own, vals.astype(jnp.float32))
    mixed = mixed + jnp.einsum('bhisj,bhsjd->bihd', w_pick, val_pick.astype(jnp.float32))
    mixed = mixed.reshape(TOKENS, WID).astype(jnp.bfloat16)
    return (h_float + jnp.dot(mixed, weight.T, preferred_element_type=jnp.float32)).astype(jnp.bfloat16)

def reference(latents, proj, temper, blocks):
    per_micro = []
    for slot in range(MICRO):
        hidden = latents[slot]
        layer_rows = []
        for depth in range(LAYERS):
            hidden = layer(hidden, proj[depth], temper[depth], blocks[slot])
            layer_rows.append(hidden)
        per_micro.append(jnp.stack(layer_rows))
    return jnp.stack(per_micro, axis=1)
```

```python
import functools
import math

import jax
import jax.numpy as jnp
from jax import lax
from jax.experimental import pallas as pl
from jax.experimental.pallas import tpu as pltpu
from jax.sharding import PartitionSpec as P

BLOCK = 64
MESH = pl.DeviceIdType.MESH
NEG = -1e30
epsilon = 1e-06
PARTS = 4
TILE = 512


def at(start, size, step):
    return pl.ds(pl.multiple_of(start, step), size)


def kernel(
    cfg, lat_ref, proj_ref, scale_ref, bias_ref, out_ref,
    weight, hidden, acc, win, mix,
    ring_send, ring_recv, pair_send, pair_recv, halo_send, halo_recv, next_send, next_recv,
):
    segs, dps, micro, toks, heads = cfg
    rows, feats = proj_ref.shape
    width = lat_ref.shape[1]
    hd = feats // heads
    part = feats // PARTS
    half = feats // 2
    tiles = width // TILE
    n = dps // 2
    seg = lax.axis_index("segment")
    dp = lax.axis_index("dp")
    chip, core = lax.div(dp, 2), lax.rem(dp, 2)
    partner = dp + 1 - 2 * core

    odd = lax.rem(chip, 2)
    pos = lax.div(chip, 2) * (1 - odd) + (n - 1 - lax.div(chip, 2)) * odd

    def pair_at(p):
        p = lax.rem(p + 2 * n, n)
        back = lax.div(p, n // 2)
        return 2 * p * (1 - back) + (2 * (n - 1 - p) + 1) * back

    up = pair_at(pos + 1) * 2 + core
    down = pair_at(pos - 1) * 2 + core

    barrier = pltpu.get_barrier_semaphore()

    def greet(s, d):
        pl.semaphore_signal(barrier, inc=1, device_id=(s, d), device_id_type=MESH)

    greet(seg, up)
    greet(seg, down)
    greet(seg, partner)
    far = dp + 2 * core - 1
    has_far = (far >= 0) & (far < dps)

    @pl.when(has_far)
    def _():
        greet(seg, far)

    @pl.when(seg > 0)
    def _():
        greet(seg - 1, dp)

    @pl.when(seg < segs - 1)
    def _():
        greet(seg + 1, dp)

    peers = 3 + has_far.astype(jnp.int32) + (seg > 0).astype(jnp.int32)
    pl.semaphore_wait(barrier, peers + (seg < segs - 1).astype(jnp.int32))

    def owner(step, q):
        return pair_at(pos - step) if q < PARTS // 2 else pair_at(pos + step)

    def block(step, q, c):
        return weight.at[at((owner(step, q) * 2 + c) * rows, rows, rows), pl.ds(q * part, part)]

    def ring_copy(step, q):
        ref = block(step, q, core)
        return pltpu.make_async_remote_copy(
            src_ref=ref, dst_ref=ref, send_sem=ring_send.at[step, q], recv_sem=ring_recv.at[step, q],
            device_id=(seg, up if q < PARTS // 2 else down), device_id_type=MESH,
        )

    def pair_copy(step, q):
        ref = block(step, q, core)
        return pltpu.make_async_remote_copy(
            src_ref=ref, dst_ref=ref, send_sem=pair_send.at[step, q], recv_sem=pair_recv.at[step, q],
            device_id=(seg, partner), device_id_type=MESH,
        )

    def ring_arrived(step, q):
        ref = block(step + 1, q, core)
        pltpu.make_async_remote_copy(
            src_ref=ref, dst_ref=ref, send_sem=ring_send.at[step, q], recv_sem=ring_recv.at[step, q],
            device_id=(seg, up if q < PARTS // 2 else down), device_id_type=MESH,
        ).wait_recv()

    def pair_arrived(step, q):
        ref = block(step, q, 1 - core)
        pltpu.make_async_remote_copy(
            src_ref=ref, dst_ref=ref, send_sem=pair_send.at[step, q], recv_sem=pair_recv.at[step, q],
            device_id=(seg, partner), device_id_type=MESH,
        ).wait_recv()

    weight[at(dp * rows, rows, rows), :] = proj_ref[...]
    for q in range(PARTS):
        ring_copy(0, q).start()
    for q in range(PARTS):
        pair_copy(0, q).start()

    @pl.when(seg == 0)
    def _():
        hidden[...] = lat_ref[...]
        acc[...] = jnp.zeros_like(acc)

    @pl.when(dp == 0)
    def _():
        for m in range(micro):
            win[m, 0:toks, :] = jnp.zeros((toks, feats), jnp.bfloat16)

    @pl.when(dp == dps - 1)
    def _():
        for m in range(micro):
            win[m, 2 * toks : 3 * toks, :] = jnp.zeros((toks, feats), jnp.bfloat16)

    deep = 2 * rows
    beside = deep % 128 == 0

    def absorb(step):
        for q in range(PARTS):
            pair_arrived(step, q)
        if beside:
            @pl.when(seg == 0)
            def _():
                for side in range(2):
                    cols = pl.ds(side * half, half)
                    there = at(owner(step, side * (PARTS // 2)) * deep, deep, deep)
                    acc[:, cols] += jnp.dot(
                        hidden[:, there], weight[there, cols], preferred_element_type=jnp.float32
                    )

    def gather_step(step, carry):
        for q in (0, PARTS // 2, 1, PARTS // 2 + 1):
            ring_arrived(step, q)

            @pl.when(step < n - 2)
            def _():
                ring_copy(step + 1, q).start()

            pair_copy(step + 1, q).start()
        absorb(step)
        return carry

    lax.fori_loop(0, n - 1, gather_step, 0)
    absorb(n - 1)

    def lines(m):
        return pl.ds(m * toks, toks)

    def project(m, arrives):
        acc[lines(m), :] = jnp.zeros((toks, feats), jnp.float32)

        def one(t, carry):
            if arrives:
                handed(m, t).wait_recv()
            cols = at(t * TILE, TILE, TILE)
            acc[lines(m), :] += jnp.dot(
                hidden[lines(m), cols], weight[cols, :], preferred_element_type=jnp.float32
            )
            return carry

        lax.fori_loop(0, tiles, one, 0)

    def handed(m, t):
        cols = at(t * TILE, TILE, TILE)
        return pltpu.make_async_remote_copy(
            src_ref=out_ref.at[lines(m), cols], dst_ref=hidden.at[lines(m), cols],
            send_sem=next_send.at[m, t], recv_sem=next_recv.at[m, t],
            device_id=(lax.rem(seg + 1, segs), dp), device_id_type=MESH,
        )

    def halo(m, way):
        there = pl.ds(0, toks) if way == 0 else pl.ds(2 * toks, toks)
        return pltpu.make_async_remote_copy(
            src_ref=win.at[m, pl.ds(toks, toks)], dst_ref=win.at[m, there],
            send_sem=halo_send.at[m, way], recv_sem=halo_recv.at[m, way],
            device_id=(seg, lax.rem(dp + (1 if way == 0 else dps - 1), dps)), device_id_type=MESH,
        )

    def share(m):
        h = hidden[lines(m), :].astype(jnp.float32)
        rate = lax.rsqrt(jnp.mean(h * h, axis=-1, keepdims=True) + epsilon)
        win[m, toks : 2 * toks, :] = (acc[lines(m), :] * rate).astype(jnp.bfloat16)

        @pl.when(dp < dps - 1)
        def _():
            halo(m, 0).start()

        @pl.when(dp > 0)
        def _():
            halo(m, 1).start()

    row_at = lax.broadcasted_iota(jnp.int32, (toks, 3 * toks), 0)
    col_at = lax.broadcasted_iota(jnp.int32, (toks, 3 * toks), 1)
    group = 3 if heads % 3 == 0 else 1

    def attend(m):
        def some(g, carry):
            for j in range(group):
                head = g * group + j
                cols = at(head * hd, hd, hd)
                vals = win[m, :, cols]
                vf = vals.astype(jnp.float32)
                keys = (
                    vf * lax.rsqrt(jnp.mean(vf * vf, axis=-1, keepdims=True) + epsilon)
                ).astype(jnp.bfloat16)
                score = lax.dot_general(
                    keys[toks : 2 * toks], keys, (((1,), (1,)), ((), ())),
                    preferred_element_type=jnp.float32,
                )
                extra = bias_ref[m, head]
                extra = jnp.concatenate(
                    [
                        jnp.broadcast_to(extra[b : b + 1], (BLOCK, 3 * toks))
                        for b in range(toks // BLOCK)
                    ],
                    axis=0,
                )
                score = score * scale_ref[head] + extra
                score = jnp.where(col_at == row_at + toks, NEG, score)
                top = jnp.max(score, axis=-1, keepdims=True)
                grown = jnp.exp(score - top)
                total = jnp.sum(grown, axis=-1, keepdims=True)
                mixed = jnp.dot(
                    grown.astype(jnp.bfloat16), vals, preferred_element_type=jnp.float32
                )
                mix[:, cols] = (mixed / total).astype(jnp.bfloat16)
            return carry

        lax.fori_loop(0, heads // group, some, 0)

    def finish(m):
        def one(t, carry):
            cols = at(t * TILE, TILE, TILE)
            back = lax.dot_general(
                mix[...], weight[cols, :], (((1,), (1,)), ((), ())),
                preferred_element_type=jnp.float32,
            )
            out_ref[lines(m), cols] = (
                hidden[lines(m), cols].astype(jnp.float32) + back
            ).astype(jnp.bfloat16)

            @pl.when(seg < segs - 1)
            def _():
                handed(m, t).start()

            return carry

        lax.fori_loop(0, tiles, one, 0)

    @pl.when(seg == 0)
    def _():
        for m in range(micro):
            if not beside:
                project(m, False)
            share(m)

    for m in range(micro):
        @pl.when(seg > 0)
        def _():
            project(m, True)
            share(m)

        @pl.when(dp > 0)
        def _():
            halo(m, 0).wait_recv()

        @pl.when(dp < dps - 1)
        def _():
            halo(m, 1).wait_recv()

        attend(m)
        finish(m)

    def settle(step, carry):
        for q in range(PARTS):
            @pl.when(step < n - 1)
            def _():
                ring_copy(step, q).wait_send()

            pair_copy(step, q).wait_send()
        return carry

    lax.fori_loop(0, n, settle, 0)
    for m in range(micro):
        @pl.when(dp < dps - 1)
        def _():
            halo(m, 0).wait_send()

        @pl.when(dp > 0)
        def _():
            halo(m, 1).wait_send()

        @pl.when(seg < segs - 1)
        def _():
            for t in range(tiles):
                handed(m, t).wait_send()


def on_device(latents, proj, temper, blocks):
    segs = lax.axis_size("segment")
    dps = lax.axis_size("dp")
    dp = lax.axis_index("dp")
    micro, toks, width = latents.shape
    heads = temper.shape[1]
    rows, feats = proj.shape[1:]
    per_dev = toks // BLOCK
    total_blocks = toks * dps // BLOCK
    seq_blocks = min(4096, toks * dps) // BLOCK
    scale = temper[0] * (1.0 / math.sqrt(feats // heads))

    query = dp * per_dev + jnp.arange(per_dev, dtype=jnp.int32)
    absolute = (dp - 1) * per_dev + blocks
    usable = (
        (absolute >= 0)
        & (absolute < total_blocks)
        & (absolute // seq_blocks == (query // seq_blocks)[None, :, None, None])
    )
    spots = jnp.arange(3 * per_dev, dtype=jnp.int32)
    listed = (blocks[..., None] == spots) & usable[..., None]
    count = jnp.sum(listed.astype(jnp.float32), axis=3)
    own = (spots[None, :] == per_dev + jnp.arange(per_dev)[:, None]).astype(jnp.float32)
    count = count + own[None, :, None, :]
    bias = jnp.where(count > 0, jnp.log(jnp.maximum(count, 1.0)), NEG)
    bias = jnp.repeat(jnp.transpose(bias, (0, 2, 1, 3)), BLOCK, axis=-1)

    n = dps // 2
    tiles = width // TILE
    dma = pltpu.SemaphoreType.DMA
    vmem = pl.BlockSpec(memory_space=pltpu.VMEM)
    states = pl.pallas_call(
        functools.partial(kernel, (segs, dps, micro, toks, heads)),
        out_shape=jax.ShapeDtypeStruct((micro * toks, width), jnp.bfloat16),
        in_specs=[vmem, vmem, pl.BlockSpec(memory_space=pltpu.SMEM), vmem],
        out_specs=vmem,
        scratch_shapes=[
            pltpu.VMEM((rows * dps, feats), jnp.bfloat16),
            pltpu.VMEM((micro * toks, width), jnp.bfloat16),
            pltpu.VMEM((micro * toks, feats), jnp.float32),
            pltpu.VMEM((micro, 3 * toks, feats), jnp.bfloat16),
            pltpu.VMEM((toks, feats), jnp.bfloat16),
            dma((n - 1, PARTS)),
            dma((n - 1, PARTS)),
            dma((n, PARTS)),
            dma((n, PARTS)),
            dma((micro, 2)),
            dma((micro, 2)),
            dma((micro, tiles)),
            dma((micro, tiles)),
        ],
        compiler_params=pltpu.CompilerParams(
            collective_id=0, has_side_effects=True, vmem_limit_bytes=48 * 1024 * 1024
        ),
        cost_estimate=pl.CostEstimate(
            flops=4 * micro * toks * width * feats,
            bytes_accessed=2 * (rows * feats + 2 * micro * toks * width),
            transcendentals=micro * heads * toks * 3 * toks,
        ),
    )(latents.reshape(micro * toks, width), proj[0], scale, bias)
    return states.reshape(1, micro, toks, width)


def solution(mesh):
    placed = (
        P(None, "dp", None),
        P("segment", "dp", None),
        P("segment", None),
        P(None, "dp", None, None),
    )
    return jax.shard_map(
        on_device,
        mesh=mesh,
        in_specs=placed,
        out_specs=P("segment", None, "dp", None),
        check_vma=False,
    )
```

```python
import functools
import math

import jax
import jax.numpy as jnp
from jax import lax
from jax.experimental import pallas as pl
from jax.experimental.pallas import tpu as pltpu
from jax.sharding import PartitionSpec as P

BLOCK = 64
MESH = pl.DeviceIdType.MESH
NEG = -1e30
epsilon = 1e-06
PARTS = 4
TILE = 512


def at(start, size, step):
    return pl.ds(pl.multiple_of(start, step), size)


def kernel(
    cfg, temper_ref, blocks_ref, lat_ref, proj_ref, out_ref,
    weight, hidden, acc, win, own_keys, mix, load_sem,
    ring_send, ring_recv, pair_send, pair_recv, halo_send, halo_recv, next_send, next_recv,
):
    segs, dps, micro, toks, heads = cfg
    rows, feats = proj_ref.shape[1:]
    width = lat_ref.shape[2]
    hd = feats // heads
    part = feats // PARTS
    half = feats // 2
    tiles = width // TILE
    n = dps // 2
    seg = lax.axis_index("segment")
    dp = lax.axis_index("dp")
    chip, core = lax.div(dp, 2), lax.rem(dp, 2)
    partner = dp + 1 - 2 * core

    odd = lax.rem(chip, 2)
    pos = lax.div(chip, 2) * (1 - odd) + (n - 1 - lax.div(chip, 2)) * odd

    def pair_at(p):
        p = lax.rem(p + 2 * n, n)
        back = lax.div(p, n // 2)
        return 2 * p * (1 - back) + (2 * (n - 1 - p) + 1) * back

    up = pair_at(pos + 1) * 2 + core
    down = pair_at(pos - 1) * 2 + core

    own_rows = pltpu.make_async_copy(
        proj_ref.at[0], weight.at[at(dp * rows, rows, rows), :], load_sem.at[0]
    )
    own_rows.start()

    def latent(m):
        return pltpu.make_async_copy(
            lat_ref.at[m], hidden.at[pl.ds(m * toks, toks)], load_sem.at[1 + m]
        )

    @pl.when(seg == 0)
    def _():
        for m in range(micro):
            latent(m).start()

    barrier = pltpu.get_barrier_semaphore()

    def greet(s, d):
        pl.semaphore_signal(barrier, inc=1, device_id=(s, d), device_id_type=MESH)

    greet(seg, up)
    greet(seg, down)
    greet(seg, partner)
    far = dp + 2 * core - 1
    has_far = (far >= 0) & (far < dps)

    @pl.when(has_far)
    def _():
        greet(seg, far)

    @pl.when(seg > 0)
    def _():
        greet(seg - 1, dp)

    @pl.when(seg < segs - 1)
    def _():
        greet(seg + 1, dp)

    peers = 3 + has_far.astype(jnp.int32) + (seg > 0).astype(jnp.int32)
    pl.semaphore_wait(barrier, peers + (seg < segs - 1).astype(jnp.int32))

    own_rows.wait()

    def owner(step, q):
        return pair_at(pos - step) if q < PARTS // 2 else pair_at(pos + step)

    def block(step, q, c):
        return weight.at[at((owner(step, q) * 2 + c) * rows, rows, rows), pl.ds(q * part, part)]

    def ring_copy(step, q):
        ref = block(step, q, core)
        return pltpu.make_async_remote_copy(
            src_ref=ref, dst_ref=ref, send_sem=ring_send.at[step, q], recv_sem=ring_recv.at[step, q],
            device_id=(seg, up if q < PARTS // 2 else down), device_id_type=MESH,
        )

    def pair_copy(step, q):
        ref = block(step, q, core)
        return pltpu.make_async_remote_copy(
            src_ref=ref, dst_ref=ref, send_sem=pair_send.at[step, q], recv_sem=pair_recv.at[step, q],
            device_id=(seg, partner), device_id_type=MESH,
        )

    def ring_arrived(step, q):
        ref = block(step + 1, q, core)
        pltpu.make_async_remote_copy(
            src_ref=ref, dst_ref=ref, send_sem=ring_send.at[step, q], recv_sem=ring_recv.at[step, q],
            device_id=(seg, up if q < PARTS // 2 else down), device_id_type=MESH,
        ).wait_recv()

    def pair_arrived(step, q):
        ref = block(step, q, 1 - core)
        pltpu.make_async_remote_copy(
            src_ref=ref, dst_ref=ref, send_sem=pair_send.at[step, q], recv_sem=pair_recv.at[step, q],
            device_id=(seg, partner), device_id_type=MESH,
        ).wait_recv()

    for q in range(PARTS):
        ring_copy(0, q).start()
    for q in range(PARTS):
        pair_copy(0, q).start()

    @pl.when(seg == 0)
    def _():
        for m in range(micro):
            latent(m).wait()
        acc[...] = jnp.zeros_like(acc)

    @pl.when(dp == 0)
    def _():
        for m in range(micro):
            win[m, 0:toks, :] = jnp.zeros((toks, feats), jnp.bfloat16)

    @pl.when(dp == dps - 1)
    def _():
        for m in range(micro):
            win[m, 2 * toks : 3 * toks, :] = jnp.zeros((toks, feats), jnp.bfloat16)

    deep = 2 * rows
    beside = deep % 128 == 0

    def absorb(step):
        for q in range(PARTS):
            pair_arrived(step, q)
        if beside:
            @pl.when(seg == 0)
            def _():
                for side in range(2):
                    cols = pl.ds(side * half, half)
                    there = at(owner(step, side * (PARTS // 2)) * deep, deep, deep)
                    acc[:, cols] += jnp.dot(
                        hidden[:, there], weight[there, cols], preferred_element_type=jnp.float32
                    )

    def gather_step(step, carry):
        for q in (0, PARTS // 2, 1, PARTS // 2 + 1):
            ring_arrived(step, q)

            @pl.when(step < n - 2)
            def _():
                ring_copy(step + 1, q).start()

            pair_copy(step + 1, q).start()
        absorb(step)
        return carry

    lax.fori_loop(0, n - 1, gather_step, 0)
    absorb(n - 1)

    def lines(m):
        return pl.ds(m * toks, toks)

    def project(m, arrives):
        acc[lines(m), :] = jnp.zeros((toks, feats), jnp.float32)

        def one(t, carry):
            if arrives:
                handed(m, t).wait_recv()
            cols = at(t * TILE, TILE, TILE)
            acc[lines(m), :] += jnp.dot(
                hidden[lines(m), cols], weight[cols, :], preferred_element_type=jnp.float32
            )
            return carry

        lax.fori_loop(0, tiles, one, 0)

    def handed(m, t):
        cols = at(t * TILE, TILE, TILE)
        return pltpu.make_async_remote_copy(
            src_ref=out_ref.at[lines(m), cols], dst_ref=hidden.at[lines(m), cols],
            send_sem=next_send.at[m, t], recv_sem=next_recv.at[m, t],
            device_id=(lax.rem(seg + 1, segs), dp), device_id_type=MESH,
        )

    def halo(m, way, piece):
        there = pl.ds(0, toks) if way == 0 else pl.ds(2 * toks, toks)
        cols = pl.ds(piece * half, half)
        return pltpu.make_async_remote_copy(
            src_ref=win.at[m, pl.ds(toks, toks), cols], dst_ref=win.at[m, there, cols],
            send_sem=halo_send.at[m, way, piece], recv_sem=halo_recv.at[m, way, piece],
            device_id=(seg, lax.rem(dp + (1 if way == 0 else dps - 1), dps)), device_id_type=MESH,
        )

    ones = jnp.ones((hd, hd), jnp.bfloat16)

    def unit(vals):
        vf = vals.astype(jnp.float32)
        squares = jnp.dot((vf * vf).astype(jnp.bfloat16), ones, preferred_element_type=jnp.float32)
        return (vf * lax.rsqrt(squares * (1.0 / hd) + epsilon)).astype(jnp.bfloat16)

    def share(m):
        h = hidden[lines(m), :].astype(jnp.float32)
        rate = lax.rsqrt(jnp.mean(h * h, axis=-1, keepdims=True) + epsilon)
        for piece in range(2):
            cols = pl.ds(piece * half, half)
            win[m, toks : 2 * toks, cols] = (acc[lines(m), cols] * rate).astype(jnp.bfloat16)

            @pl.when(dp < dps - 1)
            def _():
                halo(m, 0, piece).start()

            @pl.when(dp > 0)
            def _():
                halo(m, 1, piece).start()

    def prepare(m):
        def one(head, carry):
            cols = at(head * hd, hd, hd)
            own_keys[m, :, cols] = unit(win[m, toks : 2 * toks, cols])
            return carry

        lax.fori_loop(0, heads, one, 0)

    per_dev = toks // BLOCK
    seq_blocks = min(4096, toks * dps) // BLOCK
    diagonal = lax.broadcasted_iota(jnp.int32, (toks, toks), 0) == lax.broadcasted_iota(
        jnp.int32, (toks, toks), 1
    )
    spot = lax.div(lax.broadcasted_iota(jnp.int32, (1, 3 * toks), 1), BLOCK)
    home = lax.div(dp * per_dev, seq_blocks)
    first = home * seq_blocks - (dp - 1) * per_dev
    last = jnp.minimum((home + 1) * seq_blocks, dps * per_dev) - (dp - 1) * per_dev
    inside = (spot >= first) & (spot < last)
    group = 3 if heads % 6 == 0 else 1
    log2e = 1.4426950408889634

    def listed(m, head, b):
        count = jnp.zeros((1, 3 * toks), jnp.int32)
        for s in range(blocks_ref.shape[3]):
            count += (spot == blocks_ref[m, b, head, s]).astype(jnp.int32)
        count = jnp.where(inside, count, 0) + (spot == per_dev + b).astype(jnp.int32)
        return jnp.where(count > 0, jnp.log2(jnp.maximum(count, 1).astype(jnp.float32)), NEG)

    def attend(m):
        def one_head(head):
            cols = at(head * hd, hd, hd)
            vals = win[m, :, cols]
            query = own_keys[m, :, cols]
            keys = jnp.concatenate([unit(vals[:toks]), query, unit(vals[2 * toks :])], axis=0)
            score = lax.dot_general(
                query, keys, (((1,), (1,)), ((), ())), preferred_element_type=jnp.float32
            )
            scale = temper_ref[0, head] * (log2e / math.sqrt(hd))
            score = jnp.concatenate(
                [
                    score[b * BLOCK : (b + 1) * BLOCK] * scale + listed(m, head, b)
                    for b in range(per_dev)
                ],
                axis=0,
            )
            own = jnp.where(diagonal, NEG, score[:, toks : 2 * toks])
            score = jnp.concatenate([score[:, :toks], own, score[:, 2 * toks :]], axis=1)
            top = jnp.max(score, axis=-1, keepdims=True)
            grown = jnp.exp2(score - top).astype(jnp.bfloat16)
            wide = jnp.concatenate([vals, jnp.ones((3 * toks, hd), jnp.bfloat16)], axis=1)
            both = jnp.dot(grown, wide, preferred_element_type=jnp.float32)
            mix[m, :, cols] = (both[:, :hd] / both[:, hd:]).astype(jnp.bfloat16)

        for piece in range(2):
            @pl.when(dp > 0)
            def _():
                halo(m, 0, piece).wait_recv()

            @pl.when(dp < dps - 1)
            def _():
                halo(m, 1, piece).wait_recv()

            def some(g, carry):
                for j in range(group):
                    one_head(piece * (heads // 2) + g * group + j)
                return carry

            lax.fori_loop(0, heads // 2 // group, some, 0)

    def finish(m):
        def one(t, carry):
            cols = at(t * TILE, TILE, TILE)
            back = lax.dot_general(
                mix[m], weight[cols, :], (((1,), (1,)), ((), ())),
                preferred_element_type=jnp.float32,
            )
            out_ref[lines(m), cols] = (
                hidden[lines(m), cols].astype(jnp.float32) + back
            ).astype(jnp.bfloat16)

            @pl.when(seg < segs - 1)
            def _():
                handed(m, t).start()

            return carry

        lax.fori_loop(0, tiles, one, 0)

    @pl.when(seg == 0)
    def _():
        for m in range(micro):
            if not beside:
                project(m, False)
            share(m)
        for m in range(micro):
            prepare(m)
            attend(m)
            finish(m)

    @pl.when(seg > 0)
    def _():
        for m in range(micro):
            project(m, True)
            share(m)
            prepare(m)
            if m > 0:
                finish(m - 1)
            attend(m)
        finish(micro - 1)

    def settle(step, carry):
        for q in range(PARTS):
            @pl.when(step < n - 1)
            def _():
                ring_copy(step, q).wait_send()

            pair_copy(step, q).wait_send()
        return carry

    lax.fori_loop(0, n, settle, 0)
    for m in range(micro):
        @pl.when(dp < dps - 1)
        def _():
            for piece in range(2):
                halo(m, 0, piece).wait_send()

        @pl.when(dp > 0)
        def _():
            for piece in range(2):
                halo(m, 1, piece).wait_send()

        @pl.when(seg < segs - 1)
        def _():
            for t in range(tiles):
                handed(m, t).wait_send()


def on_device(latents, proj, temper, blocks):
    segs = lax.axis_size("segment")
    dps = lax.axis_size("dp")
    micro, toks, width = latents.shape
    heads = temper.shape[1]
    rows, feats = proj.shape[1:]
    n = dps // 2
    tiles = width // TILE
    dma = pltpu.SemaphoreType.DMA
    vmem = pl.BlockSpec(memory_space=pltpu.VMEM)
    smem = pl.BlockSpec(memory_space=pltpu.SMEM)
    anywhere = pl.BlockSpec(memory_space=pl.ANY)
    states = pl.pallas_call(
        functools.partial(kernel, (segs, dps, micro, toks, heads)),
        out_shape=jax.ShapeDtypeStruct((micro * toks, width), jnp.bfloat16),
        in_specs=[smem, smem, anywhere, anywhere],
        out_specs=vmem,
        scratch_shapes=[
            pltpu.VMEM((rows * dps, feats), jnp.bfloat16),
            pltpu.VMEM((micro * toks, width), jnp.bfloat16),
            pltpu.VMEM((micro * toks, feats), jnp.float32),
            pltpu.VMEM((micro, 3 * toks, feats), jnp.bfloat16),
            pltpu.VMEM((micro, toks, feats), jnp.bfloat16),
            pltpu.VMEM((micro, toks, feats), jnp.bfloat16),
            dma((1 + micro,)),
            dma((n - 1, PARTS)),
            dma((n - 1, PARTS)),
            dma((n, PARTS)),
            dma((n, PARTS)),
            dma((micro, 2, 2)),
            dma((micro, 2, 2)),
            dma((micro, tiles)),
            dma((micro, tiles)),
        ],
        compiler_params=pltpu.CompilerParams(
            collective_id=0, has_side_effects=True, vmem_limit_bytes=62 * 1024 * 1024
        ),
        cost_estimate=pl.CostEstimate(
            flops=4 * micro * toks * width * feats,
            bytes_accessed=2 * (rows * feats + 2 * micro * toks * width),
            transcendentals=micro * heads * toks * 3 * toks,
        ),
    )(temper, blocks, latents, proj)
    return states.reshape(1, micro, toks, width)


def solution(mesh):
    placed = (
        P(None, "dp", None),
        P("segment", "dp", None),
        P("segment", None),
        P(None, "dp", None, None),
    )
    return jax.shard_map(
        on_device,
        mesh=mesh,
        in_specs=placed,
        out_specs=P("segment", None, "dp", None),
        check_vma=False,
    )
```

```python
import functools
import math

import jax
import jax.numpy as jnp
from jax import lax
from jax.experimental import pallas as pl
from jax.experimental.pallas import tpu as pltpu
from jax.sharding import PartitionSpec as P

BLOCK = 64
MESH = pl.DeviceIdType.MESH
NEG = -1e30
epsilon = 1e-06
PARTS = 4
TILE = 512


def at(start, size, step):
    return pl.ds(pl.multiple_of(start, step), size)


def kernel(
    cfg, temper_ref, blocks_ref, lat_ref, proj_ref, out_ref,
    weight, hidden, acc, win, own_keys, mix, load_sem,
    ring_send, ring_recv, pair_send, pair_recv, halo_send, halo_recv, next_send, next_recv,
):
    segs, dps, micro, toks, heads = cfg
    rows, feats = proj_ref.shape[1:]
    width = lat_ref.shape[2]
    hd = feats // heads
    part = feats // PARTS
    half = feats // 2
    tiles = width // TILE
    n = dps // 2
    seg = lax.axis_index("segment")
    dp = lax.axis_index("dp")
    chip, core = lax.div(dp, 2), lax.rem(dp, 2)
    partner = dp + 1 - 2 * core

    odd = lax.rem(chip, 2)
    pos = lax.div(chip, 2) * (1 - odd) + (n - 1 - lax.div(chip, 2)) * odd

    def pair_at(p):
        p = lax.rem(p + 2 * n, n)
        back = lax.div(p, n // 2)
        return 2 * p * (1 - back) + (2 * (n - 1 - p) + 1) * back

    up = pair_at(pos + 1) * 2 + core
    down = pair_at(pos - 1) * 2 + core

    own_rows = pltpu.make_async_copy(
        proj_ref.at[0], weight.at[at(dp * rows, rows, rows), :], load_sem.at[0]
    )
    own_rows.start()

    def latent(m):
        return pltpu.make_async_copy(
            lat_ref.at[m], hidden.at[pl.ds(m * toks, toks)], load_sem.at[1 + m]
        )

    @pl.when(seg == 0)
    def _():
        for m in range(micro):
            latent(m).start()

    barrier = pltpu.get_barrier_semaphore()

    def greet(s, d):
        pl.semaphore_signal(barrier, inc=1, device_id=(s, d), device_id_type=MESH)

    greet(seg, up)
    greet(seg, down)
    greet(seg, partner)
    far = dp + 2 * core - 1
    has_far = (far >= 0) & (far < dps)

    @pl.when(has_far)
    def _():
        greet(seg, far)

    @pl.when(seg > 0)
    def _():
        greet(seg - 1, dp)

    @pl.when(seg < segs - 1)
    def _():
        greet(seg + 1, dp)

    peers = 3 + has_far.astype(jnp.int32) + (seg > 0).astype(jnp.int32)
    pl.semaphore_wait(barrier, peers + (seg < segs - 1).astype(jnp.int32))

    own_rows.wait()

    def owner(step, q):
        return pair_at(pos - step) if q < PARTS // 2 else pair_at(pos + step)

    def block(step, q, c):
        return weight.at[at((owner(step, q) * 2 + c) * rows, rows, rows), pl.ds(q * part, part)]

    def ring_copy(step, q):
        ref = block(step, q, core)
        return pltpu.make_async_remote_copy(
            src_ref=ref, dst_ref=ref, send_sem=ring_send.at[step, q], recv_sem=ring_recv.at[step, q],
            device_id=(seg, up if q < PARTS // 2 else down), device_id_type=MESH,
        )

    def pair_copy(step, q):
        ref = block(step, q, core)
        return pltpu.make_async_remote_copy(
            src_ref=ref, dst_ref=ref, send_sem=pair_send.at[step, q], recv_sem=pair_recv.at[step, q],
            device_id=(seg, partner), device_id_type=MESH,
        )

    def ring_arrived(step, q):
        ref = block(step + 1, q, core)
        pltpu.make_async_remote_copy(
            src_ref=ref, dst_ref=ref, send_sem=ring_send.at[step, q], recv_sem=ring_recv.at[step, q],
            device_id=(seg, up if q < PARTS // 2 else down), device_id_type=MESH,
        ).wait_recv()

    def pair_arrived(step, q):
        ref = block(step, q, 1 - core)
        pltpu.make_async_remote_copy(
            src_ref=ref, dst_ref=ref, send_sem=pair_send.at[step, q], recv_sem=pair_recv.at[step, q],
            device_id=(seg, partner), device_id_type=MESH,
        ).wait_recv()

    for q in range(PARTS):
        ring_copy(0, q).start()
    for q in range(PARTS):
        pair_copy(0, q).start()

    @pl.when(seg == 0)
    def _():
        for m in range(micro):
            latent(m).wait()
        acc[...] = jnp.zeros_like(acc)

    @pl.when(dp == 0)
    def _():
        for m in range(micro):
            win[m, 0:toks, :] = jnp.zeros((toks, feats), jnp.bfloat16)

    @pl.when(dp == dps - 1)
    def _():
        for m in range(micro):
            win[m, 2 * toks : 3 * toks, :] = jnp.zeros((toks, feats), jnp.bfloat16)

    deep = 2 * rows
    beside = deep % 128 == 0

    def absorb(step):
        for q in range(PARTS):
            pair_arrived(step, q)
        if beside:
            @pl.when(seg == 0)
            def _():
                for side in range(2):
                    cols = pl.ds(side * half, half)
                    there = at(owner(step, side * (PARTS // 2)) * deep, deep, deep)
                    acc[:, cols] += jnp.dot(
                        hidden[:, there], weight[there, cols], preferred_element_type=jnp.float32
                    )

    def gather_step(step, carry):
        for q in (0, PARTS // 2, 1, PARTS // 2 + 1):
            ring_arrived(step, q)

            @pl.when(step < n - 2)
            def _():
                ring_copy(step + 1, q).start()

            pair_copy(step + 1, q).start()
        absorb(step)
        return carry

    lax.fori_loop(0, n - 1, gather_step, 0)
    absorb(n - 1)

    def lines(m):
        return pl.ds(m * toks, toks)

    lead = 4 * tiles // 6

    def project(m, arrives):
        acc[lines(m), :] = jnp.zeros((toks, feats), jnp.float32)

        def one(finishing, t, carry):
            if finishing:
                finish_piece(m - 1, t)
            if arrives:
                handed(m, t).wait_recv()
            cols = at(t * TILE, TILE, TILE)
            acc[lines(m), :] += jnp.dot(
                hidden[lines(m), cols], weight[cols, :], preferred_element_type=jnp.float32
            )
            return carry

        if arrives and m > 0:
            lax.fori_loop(0, lead, functools.partial(one, True), 0)
            lax.fori_loop(lead, tiles, functools.partial(one, False), 0)
        else:
            lax.fori_loop(0, tiles, functools.partial(one, False), 0)

    def handed(m, t):
        cols = at(t * TILE, TILE, TILE)
        return pltpu.make_async_remote_copy(
            src_ref=out_ref.at[lines(m), cols], dst_ref=hidden.at[lines(m), cols],
            send_sem=next_send.at[m, t], recv_sem=next_recv.at[m, t],
            device_id=(lax.rem(seg + 1, segs), dp), device_id_type=MESH,
        )

    def halo(m, way, piece):
        there = pl.ds(0, toks) if way == 0 else pl.ds(2 * toks, toks)
        cols = pl.ds(piece * half, half)
        return pltpu.make_async_remote_copy(
            src_ref=win.at[m, pl.ds(toks, toks), cols], dst_ref=win.at[m, there, cols],
            send_sem=halo_send.at[m, way, piece], recv_sem=halo_recv.at[m, way, piece],
            device_id=(seg, lax.rem(dp + (1 if way == 0 else dps - 1), dps)), device_id_type=MESH,
        )

    ones = jnp.ones((hd, hd), jnp.bfloat16)

    def unit(vals):
        vf = vals.astype(jnp.float32)
        squares = jnp.dot((vf * vf).astype(jnp.bfloat16), ones, preferred_element_type=jnp.float32)
        return (vf * lax.rsqrt(squares * (1.0 / hd) + epsilon)).astype(jnp.bfloat16)

    def share(m):
        h = hidden[lines(m), :].astype(jnp.float32)
        rate = lax.rsqrt(jnp.mean(h * h, axis=-1, keepdims=True) + epsilon)
        for piece in range(2):
            cols = pl.ds(piece * half, half)
            win[m, toks : 2 * toks, cols] = (acc[lines(m), cols] * rate).astype(jnp.bfloat16)

            @pl.when(dp < dps - 1)
            def _():
                halo(m, 0, piece).start()

            @pl.when(dp > 0)
            def _():
                halo(m, 1, piece).start()

    def prepare(m):
        def one(head, carry):
            cols = at(head * hd, hd, hd)
            own_keys[m, :, cols] = unit(win[m, toks : 2 * toks, cols])
            return carry

        lax.fori_loop(0, heads, one, 0)

    per_dev = toks // BLOCK
    seq_blocks = min(4096, toks * dps) // BLOCK
    diagonal = lax.broadcasted_iota(jnp.int32, (toks, toks), 0) == lax.broadcasted_iota(
        jnp.int32, (toks, toks), 1
    )
    spot = lax.div(lax.broadcasted_iota(jnp.int32, (1, 3 * toks), 1), BLOCK)
    home = lax.div(dp * per_dev, seq_blocks)
    first = home * seq_blocks - (dp - 1) * per_dev
    last = jnp.minimum((home + 1) * seq_blocks, dps * per_dev) - (dp - 1) * per_dev
    inside = (spot >= first) & (spot < last)
    group = 3 if heads % 6 == 0 else 1
    log2e = 1.4426950408889634

    def listed(m, head, b):
        count = jnp.zeros((1, 3 * toks), jnp.int32)
        for s in range(blocks_ref.shape[3]):
            count += (spot == blocks_ref[m, b, head, s]).astype(jnp.int32)
        count = jnp.where(inside, count, 0) + (spot == per_dev + b).astype(jnp.int32)
        return jnp.where(count > 0, jnp.log2(jnp.maximum(count, 1).astype(jnp.float32)), NEG)

    def attend(m):
        def one_head(head):
            cols = at(head * hd, hd, hd)
            vals = win[m, :, cols]
            query = own_keys[m, :, cols]
            keys = jnp.concatenate([unit(vals[:toks]), query, unit(vals[2 * toks :])], axis=0)
            score = lax.dot_general(
                query, keys, (((1,), (1,)), ((), ())), preferred_element_type=jnp.float32
            )
            scale = temper_ref[0, head] * (log2e / math.sqrt(hd))
            score = jnp.concatenate(
                [
                    score[b * BLOCK : (b + 1) * BLOCK] * scale + listed(m, head, b)
                    for b in range(per_dev)
                ],
                axis=0,
            )
            own = jnp.where(diagonal, NEG, score[:, toks : 2 * toks])
            score = jnp.concatenate([score[:, :toks], own, score[:, 2 * toks :]], axis=1)
            top = jnp.max(score, axis=-1, keepdims=True)
            grown = jnp.exp2(score - top).astype(jnp.bfloat16)
            wide = jnp.concatenate([vals, jnp.ones((3 * toks, hd), jnp.bfloat16)], axis=1)
            both = jnp.dot(grown, wide, preferred_element_type=jnp.float32)
            mix[m, :, cols] = (both[:, :hd] / both[:, hd:]).astype(jnp.bfloat16)

        for piece in range(2):
            @pl.when(dp > 0)
            def _():
                halo(m, 0, piece).wait_recv()

            @pl.when(dp < dps - 1)
            def _():
                halo(m, 1, piece).wait_recv()

            def some(g, carry):
                for j in range(group):
                    one_head(piece * (heads // 2) + g * group + j)
                return carry

            lax.fori_loop(0, heads // 2 // group, some, 0)

    def finish_piece(m, t):
        cols = at(t * TILE, TILE, TILE)
        back = lax.dot_general(
            mix[m], weight[cols, :], (((1,), (1,)), ((), ())),
            preferred_element_type=jnp.float32,
        )
        out_ref[lines(m), cols] = (
            hidden[lines(m), cols].astype(jnp.float32) + back
        ).astype(jnp.bfloat16)

        @pl.when(seg < segs - 1)
        def _():
            handed(m, t).start()

    def finish(m, begin=0):
        def one(t, carry):
            finish_piece(m, t)
            return carry

        lax.fori_loop(begin, tiles, one, 0)

    @pl.when(seg == 0)
    def _():
        for m in range(micro):
            if not beside:
                project(m, False)
            share(m)
        for m in range(micro):
            prepare(m)
            attend(m)
            finish(m)

    @pl.when(seg > 0)
    def _():
        for m in range(micro):
            project(m, True)
            share(m)
            prepare(m)
            if m > 0:
                finish(m - 1, lead)
            attend(m)
        finish(micro - 1)

    def settle(step, carry):
        for q in range(PARTS):
            @pl.when(step < n - 1)
            def _():
                ring_copy(step, q).wait_send()

            pair_copy(step, q).wait_send()
        return carry

    lax.fori_loop(0, n, settle, 0)
    for m in range(micro):
        @pl.when(dp < dps - 1)
        def _():
            for piece in range(2):
                halo(m, 0, piece).wait_send()

        @pl.when(dp > 0)
        def _():
            for piece in range(2):
                halo(m, 1, piece).wait_send()

        @pl.when(seg < segs - 1)
        def _():
            for t in range(tiles):
                handed(m, t).wait_send()


def on_device(latents, proj, temper, blocks):
    segs = lax.axis_size("segment")
    dps = lax.axis_size("dp")
    micro, toks, width = latents.shape
    heads = temper.shape[1]
    rows, feats = proj.shape[1:]
    n = dps // 2
    tiles = width // TILE
    dma = pltpu.SemaphoreType.DMA
    vmem = pl.BlockSpec(memory_space=pltpu.VMEM)
    smem = pl.BlockSpec(memory_space=pltpu.SMEM)
    anywhere = pl.BlockSpec(memory_space=pl.ANY)
    states = pl.pallas_call(
        functools.partial(kernel, (segs, dps, micro, toks, heads)),
        out_shape=jax.ShapeDtypeStruct((micro * toks, width), jnp.bfloat16),
        in_specs=[smem, smem, anywhere, anywhere],
        out_specs=vmem,
        scratch_shapes=[
            pltpu.VMEM((rows * dps, feats), jnp.bfloat16),
            pltpu.VMEM((micro * toks, width), jnp.bfloat16),
            pltpu.VMEM((micro * toks, feats), jnp.float32),
            pltpu.VMEM((micro, 3 * toks, feats), jnp.bfloat16),
            pltpu.VMEM((micro, toks, feats), jnp.bfloat16),
            pltpu.VMEM((micro, toks, feats), jnp.bfloat16),
            dma((1 + micro,)),
            dma((n - 1, PARTS)),
            dma((n - 1, PARTS)),
            dma((n, PARTS)),
            dma((n, PARTS)),
            dma((micro, 2, 2)),
            dma((micro, 2, 2)),
            dma((micro, tiles)),
            dma((micro, tiles)),
        ],
        compiler_params=pltpu.CompilerParams(
            collective_id=0, has_side_effects=True, vmem_limit_bytes=62 * 1024 * 1024
        ),
        cost_estimate=pl.CostEstimate(
            flops=4 * micro * toks * width * feats,
            bytes_accessed=2 * (rows * feats + 2 * micro * toks * width),
            transcendentals=micro * heads * toks * 3 * toks,
        ),
    )(temper, blocks, latents, proj)
    return states.reshape(1, micro, toks, width)


def solution(mesh):
    placed = (
        P(None, "dp", None),
        P("segment", "dp", None),
        P("segment", None),
        P(None, "dp", None, None),
    )
    return jax.shard_map(
        on_device,
        mesh=mesh,
        in_specs=placed,
        out_specs=P("segment", None, "dp", None),
        check_vma=False,
    )
```

```python
import functools
import math

import jax
import jax.numpy as jnp
from jax import lax
from jax.experimental import pallas as pl
from jax.experimental.pallas import tpu as pltpu
from jax.sharding import PartitionSpec as P

BLOCK = 64
MESH = pl.DeviceIdType.MESH
NEG = -1e30
epsilon = 1e-06
PARTS = 4
TILE = 512


def at(start, size, step):
    return pl.ds(pl.multiple_of(start, step), size)


def kernel(
    cfg, temper_ref, blocks_ref, lat_ref, proj_ref, out_ref,
    weight, hidden, acc, win, own_keys, mix, load_sem,
    ring_send, ring_recv, pair_send, pair_recv, halo_send, halo_recv, next_send, next_recv,
):
    segs, dps, micro, toks, heads = cfg
    rows, feats = proj_ref.shape[1:]
    width = lat_ref.shape[2]
    hd = feats // heads
    part = feats // PARTS
    half = feats // 2
    tiles = width // TILE
    n = dps // 2
    seg = lax.axis_index("segment")
    dp = lax.axis_index("dp")
    chip, core = lax.div(dp, 2), lax.rem(dp, 2)
    partner = dp + 1 - 2 * core

    odd = lax.rem(chip, 2)
    pos = lax.div(chip, 2) * (1 - odd) + (n - 1 - lax.div(chip, 2)) * odd

    def pair_at(p):
        p = lax.rem(p + 2 * n, n)
        back = lax.div(p, n // 2)
        return 2 * p * (1 - back) + (2 * (n - 1 - p) + 1) * back

    up = pair_at(pos + 1) * 2 + core
    down = pair_at(pos - 1) * 2 + core

    own_rows = pltpu.make_async_copy(
        proj_ref.at[0], weight.at[at(dp * rows, rows, rows), :], load_sem.at[0]
    )
    own_rows.start()

    def latent(m):
        return pltpu.make_async_copy(
            lat_ref.at[m], hidden.at[pl.ds(m * toks, toks)], load_sem.at[1 + m]
        )

    @pl.when(seg == 0)
    def _():
        for m in range(micro):
            latent(m).start()

    barrier = pltpu.get_barrier_semaphore()

    def greet(s, d):
        pl.semaphore_signal(barrier, inc=1, device_id=(s, d), device_id_type=MESH)

    greet(seg, up)
    greet(seg, down)
    greet(seg, partner)
    far = dp + 2 * core - 1
    has_far = (far >= 0) & (far < dps)

    @pl.when(has_far)
    def _():
        greet(seg, far)

    @pl.when(seg > 0)
    def _():
        greet(seg - 1, dp)

    @pl.when(seg < segs - 1)
    def _():
        greet(seg + 1, dp)

    peers = 3 + has_far.astype(jnp.int32) + (seg > 0).astype(jnp.int32)
    pl.semaphore_wait(barrier, peers + (seg < segs - 1).astype(jnp.int32))

    own_rows.wait()

    def owner(step, q):
        return pair_at(pos - step) if q < PARTS // 2 else pair_at(pos + step)

    def block(step, q, c):
        return weight.at[at((owner(step, q) * 2 + c) * rows, rows, rows), pl.ds(q * part, part)]

    def ring_copy(step, q):
        ref = block(step, q, core)
        return pltpu.make_async_remote_copy(
            src_ref=ref, dst_ref=ref, send_sem=ring_send.at[step, q], recv_sem=ring_recv.at[step, q],
            device_id=(seg, up if q < PARTS // 2 else down), device_id_type=MESH,
        )

    def pair_copy(step, q):
        ref = block(step, q, core)
        return pltpu.make_async_remote_copy(
            src_ref=ref, dst_ref=ref, send_sem=pair_send.at[step, q], recv_sem=pair_recv.at[step, q],
            device_id=(seg, partner), device_id_type=MESH,
        )

    def ring_arrived(step, q):
        ref = block(step + 1, q, core)
        pltpu.make_async_remote_copy(
            src_ref=ref, dst_ref=ref, send_sem=ring_send.at[step, q], recv_sem=ring_recv.at[step, q],
            device_id=(seg, up if q < PARTS // 2 else down), device_id_type=MESH,
        ).wait_recv()

    def pair_arrived(step, q):
        ref = block(step, q, 1 - core)
        pltpu.make_async_remote_copy(
            src_ref=ref, dst_ref=ref, send_sem=pair_send.at[step, q], recv_sem=pair_recv.at[step, q],
            device_id=(seg, partner), device_id_type=MESH,
        ).wait_recv()

    for q in range(PARTS):
        ring_copy(0, q).start()
    for q in range(PARTS):
        pair_copy(0, q).start()

    @pl.when(seg == 0)
    def _():
        for m in range(micro):
            latent(m).wait()
        acc[...] = jnp.zeros_like(acc)

    @pl.when(dp == 0)
    def _():
        for m in range(micro):
            win[m, 0:toks, :] = jnp.zeros((toks, feats), jnp.bfloat16)

    @pl.when(dp == dps - 1)
    def _():
        for m in range(micro):
            win[m, 2 * toks : 3 * toks, :] = jnp.zeros((toks, feats), jnp.bfloat16)

    deep = 2 * rows
    beside = deep % 128 == 0

    def absorb(step):
        for q in range(PARTS):
            pair_arrived(step, q)
        if beside:
            @pl.when(seg == 0)
            def _():
                for side in range(2):
                    cols = pl.ds(side * half, half)
                    there = at(owner(step, side * (PARTS // 2)) * deep, deep, deep)
                    acc[:, cols] += jnp.dot(
                        hidden[:, there], weight[there, cols], preferred_element_type=jnp.float32
                    )

    def gather_step(step, carry):
        for q in (0, PARTS // 2, 1, PARTS // 2 + 1):
            ring_arrived(step, q)

            @pl.when(step < n - 2)
            def _():
                ring_copy(step + 1, q).start()

            pair_copy(step + 1, q).start()
        absorb(step)
        return carry

    lax.fori_loop(0, n - 1, gather_step, 0)
    absorb(n - 1)

    def lines(m):
        return pl.ds(m * toks, toks)

    def project(m, arrives):
        acc[lines(m), :] = jnp.zeros((toks, feats), jnp.float32)

        def one(t, carry):
            if arrives:
                handed(m, t).wait_recv()
            cols = at(t * TILE, TILE, TILE)
            acc[lines(m), :] += jnp.dot(
                hidden[lines(m), cols], weight[cols, :], preferred_element_type=jnp.float32
            )
            return carry

        lax.fori_loop(0, tiles, one, 0)

    def handed(m, t):
        cols = at(t * TILE, TILE, TILE)
        return pltpu.make_async_remote_copy(
            src_ref=out_ref.at[lines(m), cols], dst_ref=hidden.at[lines(m), cols],
            send_sem=next_send.at[m, t], recv_sem=next_recv.at[m, t],
            device_id=(lax.rem(seg + 1, segs), dp), device_id_type=MESH,
        )

    def halo(m, way, piece):
        there = pl.ds(0, toks) if way == 0 else pl.ds(2 * toks, toks)
        cols = pl.ds(piece * half, half)
        return pltpu.make_async_remote_copy(
            src_ref=win.at[m, pl.ds(toks, toks), cols], dst_ref=win.at[m, there, cols],
            send_sem=halo_send.at[m, way, piece], recv_sem=halo_recv.at[m, way, piece],
            device_id=(seg, lax.rem(dp + (1 if way == 0 else dps - 1), dps)), device_id_type=MESH,
        )

    ones = jnp.ones((hd, hd), jnp.bfloat16)

    def unit(vals):
        vf = vals.astype(jnp.float32)
        squares = jnp.dot((vf * vf).astype(jnp.bfloat16), ones, preferred_element_type=jnp.float32)
        return (vf * lax.rsqrt(squares * (1.0 / hd) + epsilon)).astype(jnp.bfloat16)

    def share(m):
        h = hidden[lines(m), :].astype(jnp.float32)
        rate = lax.rsqrt(jnp.mean(h * h, axis=-1, keepdims=True) + epsilon)
        for piece in range(2):
            cols = pl.ds(piece * half, half)
            win[m, toks : 2 * toks, cols] = (acc[lines(m), cols] * rate).astype(jnp.bfloat16)

            @pl.when(dp < dps - 1)
            def _():
                halo(m, 0, piece).start()

            @pl.when(dp > 0)
            def _():
                halo(m, 1, piece).start()

    def prepare(m):
        def one(head, carry):
            cols = at(head * hd, hd, hd)
            own_keys[m, :, cols] = unit(win[m, toks : 2 * toks, cols])
            return carry

        lax.fori_loop(0, heads, one, 0)

    per_dev = toks // BLOCK
    seq_blocks = min(4096, toks * dps) // BLOCK
    diagonal = lax.broadcasted_iota(jnp.int32, (toks, toks), 0) == lax.broadcasted_iota(
        jnp.int32, (toks, toks), 1
    )
    spot = lax.div(lax.broadcasted_iota(jnp.int32, (1, 3 * toks), 1), BLOCK)
    home = lax.div(dp * per_dev, seq_blocks)
    first = home * seq_blocks - (dp - 1) * per_dev
    last = jnp.minimum((home + 1) * seq_blocks, dps * per_dev) - (dp - 1) * per_dev
    inside = (spot >= first) & (spot < last)
    group = 3 if heads % 6 == 0 else 1
    log2e = 1.4426950408889634

    def listed(m, head, b):
        count = jnp.zeros((1, 3 * toks), jnp.int32)
        for s in range(blocks_ref.shape[3]):
            count += (spot == blocks_ref[m, b, head, s]).astype(jnp.int32)
        count = jnp.where(inside, count, 0) + (spot == per_dev + b).astype(jnp.int32)
        return jnp.where(count > 0, jnp.log2(jnp.maximum(count, 1).astype(jnp.float32)), NEG)

    def attend(m):
        def one_head(head):
            cols = at(head * hd, hd, hd)
            vals = win[m, :, cols]
            query = own_keys[m, :, cols]
            keys = jnp.concatenate([unit(vals[:toks]), query, unit(vals[2 * toks :])], axis=0)
            score = lax.dot_general(
                query, keys, (((1,), (1,)), ((), ())), preferred_element_type=jnp.float32
            )
            scale = temper_ref[0, head] * (log2e / math.sqrt(hd))
            score = jnp.concatenate(
                [
                    score[b * BLOCK : (b + 1) * BLOCK] * scale + listed(m, head, b)
                    for b in range(per_dev)
                ],
                axis=0,
            )
            own = jnp.where(diagonal, NEG, score[:, toks : 2 * toks])
            score = jnp.concatenate([score[:, :toks], own, score[:, 2 * toks :]], axis=1)
            top = jnp.max(score, axis=-1, keepdims=True)
            grown = jnp.exp2(score - top).astype(jnp.bfloat16)
            wide = jnp.concatenate([vals, jnp.ones((3 * toks, hd), jnp.bfloat16)], axis=1)
            both = jnp.dot(grown, wide, preferred_element_type=jnp.float32)
            mix[m, :, cols] = (both[:, :hd] / both[:, hd:]).astype(jnp.bfloat16)

        for piece in range(2):
            @pl.when(dp > 0)
            def _():
                halo(m, 0, piece).wait_recv()

            @pl.when(dp < dps - 1)
            def _():
                halo(m, 1, piece).wait_recv()

            def some(g, carry):
                for j in range(group):
                    one_head(piece * (heads // 2) + g * group + j)
                return carry

            lax.fori_loop(0, heads // 2 // group, some, 0)

    def finish(m, begin=0, end=tiles):
        def one(t, carry):
            cols = at(t * TILE, TILE, TILE)
            back = lax.dot_general(
                mix[m], weight[cols, :], (((1,), (1,)), ((), ())),
                preferred_element_type=jnp.float32,
            )
            out_ref[lines(m), cols] = (
                hidden[lines(m), cols].astype(jnp.float32) + back
            ).astype(jnp.bfloat16)

            @pl.when(seg < segs - 1)
            def _():
                handed(m, t).start()

            return carry

        lax.fori_loop(begin, end, one, 0)

    lead = 2

    def finish_two(begin):
        both = pl.ds((micro - 2) * toks, 2 * toks)
        mixed = mix[micro - 2 : micro].reshape(2 * toks, feats)

        def one(t, carry):
            cols = at(t * TILE, TILE, TILE)
            back = lax.dot_general(
                mixed, weight[cols, :], (((1,), (1,)), ((), ())),
                preferred_element_type=jnp.float32,
            )
            out_ref[both, cols] = (hidden[both, cols].astype(jnp.float32) + back).astype(
                jnp.bfloat16
            )
            return carry

        lax.fori_loop(begin, tiles, one, 0)

    @pl.when(seg == 0)
    def _():
        for m in range(micro):
            if not beside:
                project(m, False)
            share(m)
        for m in range(micro):
            prepare(m)
            attend(m)
            finish(m)

    @pl.when(seg > 0)
    def _():
        for m in range(micro):
            project(m, True)
            share(m)
            prepare(m)
            if 0 < m < micro - 1:
                finish(m - 1)
            elif m > 0:
                finish(m - 1, 0, lead)

                @pl.when(seg < segs - 1)
                def _():
                    finish(m - 1, lead)

            attend(m)
        if micro > 1:
            @pl.when(seg < segs - 1)
            def _():
                finish(micro - 1)

            @pl.when(seg == segs - 1)
            def _():
                finish_two(lead)
                finish(micro - 1, 0, lead)
        else:
            finish(0)

    def settle(step, carry):
        for q in range(PARTS):
            @pl.when(step < n - 1)
            def _():
                ring_copy(step, q).wait_send()

            pair_copy(step, q).wait_send()
        return carry

    lax.fori_loop(0, n, settle, 0)
    for m in range(micro):
        @pl.when(dp < dps - 1)
        def _():
            for piece in range(2):
                halo(m, 0, piece).wait_send()

        @pl.when(dp > 0)
        def _():
            for piece in range(2):
                halo(m, 1, piece).wait_send()

        @pl.when(seg < segs - 1)
        def _():
            for t in range(tiles):
                handed(m, t).wait_send()


def on_device(latents, proj, temper, blocks):
    segs = lax.axis_size("segment")
    dps = lax.axis_size("dp")
    micro, toks, width = latents.shape
    heads = temper.shape[1]
    rows, feats = proj.shape[1:]
    n = dps // 2
    tiles = width // TILE
    dma = pltpu.SemaphoreType.DMA
    vmem = pl.BlockSpec(memory_space=pltpu.VMEM)
    smem = pl.BlockSpec(memory_space=pltpu.SMEM)
    anywhere = pl.BlockSpec(memory_space=pl.ANY)
    states = pl.pallas_call(
        functools.partial(kernel, (segs, dps, micro, toks, heads)),
        out_shape=jax.ShapeDtypeStruct((micro * toks, width), jnp.bfloat16),
        in_specs=[smem, smem, anywhere, anywhere],
        out_specs=vmem,
        scratch_shapes=[
            pltpu.VMEM((rows * dps, feats), jnp.bfloat16),
            pltpu.VMEM((micro * toks, width), jnp.bfloat16),
            pltpu.VMEM((micro * toks, feats), jnp.float32),
            pltpu.VMEM((micro, 3 * toks, feats), jnp.bfloat16),
            pltpu.VMEM((micro, toks, feats), jnp.bfloat16),
            pltpu.VMEM((micro, toks, feats), jnp.bfloat16),
            dma((1 + micro,)),
            dma((n - 1, PARTS)),
            dma((n - 1, PARTS)),
            dma((n, PARTS)),
            dma((n, PARTS)),
            dma((micro, 2, 2)),
            dma((micro, 2, 2)),
            dma((micro, tiles)),
            dma((micro, tiles)),
        ],
        compiler_params=pltpu.CompilerParams(
            collective_id=0, has_side_effects=True, vmem_limit_bytes=62 * 1024 * 1024
        ),
        cost_estimate=pl.CostEstimate(
            flops=4 * micro * toks * width * feats,
            bytes_accessed=2 * (rows * feats + 2 * micro * toks * width),
            transcendentals=micro * heads * toks * 3 * toks,
        ),
    )(temper, blocks, latents, proj)
    return states.reshape(1, micro, toks, width)


def solution(mesh):
    placed = (
        P(None, "dp", None),
        P("segment", "dp", None),
        P("segment", None),
        P(None, "dp", None, None),
    )
    return jax.shard_map(
        on_device,
        mesh=mesh,
        in_specs=placed,
        out_specs=P("segment", None, "dp", None),
        check_vma=False,
    )
```
